32 devices in a mesh: doc: 16 (over z, y, core), head: 2 (over x).
Axes of the slice: x: 2, y: 2, z: 4, core: 2. Of those that a mesh axis runs over, the one named last changes fastest.
Arguments:
- queries: bfloat16 [8192, 4096], P('doc', 'head'), may hold values from -6 to 6
- local_keys: bfloat16 [8192, 4096], P('doc', 'head'), may hold values from -6 to 6
- local_values: bfloat16 [8192, 4096], P('doc', 'head'), may hold values from -6 to 6
- mem_keys: bfloat16 [16384, 4096], P('doc', 'head'), may hold values from -6 to 6
- mem_values: bfloat16 [16384, 4096], P('doc', 'head'), may hold values from -6 to 6
- offsets: int32 [16, 4], P('doc'), may hold values from 1 to 4
- mem_lengths: int32 [16], replicated, may hold values from 1 to 1024
- out_weight: bfloat16 [4096, 2048], P('head'), may hold values from -0.09375 to 0.09375
Outputs:
- mixed: bfloat16 [8192, 2048], P(('doc', 'head'))
The draws below stay inside these ranges and needn't reach their ends.
All inputs are finite; a program needn't handle non-finite values.
Results may differ from the reference program's by a relative error of at most 0.015.
Values may be sent and summed in bfloat16 or wider, within the bound.
A program may use at most 320 MiB of HBM per device.

```python
import math
import jax
import jax.numpy as jnp
from jax import lax

HEADS = 32
DH = 128
OUT = 2048
SLOTS = 4
QUERIES = 512
MEM = 1024
DOCS = 16


def draw_queries(key, part):
    full_shape = (DOCS * QUERIES, HEADS * DH)
    drawn = jnp.clip(jax.random.normal(jax.random.fold_in(key, 21), full_shape, jnp.float32), -6.0, 6.0)
    return drawn.astype(jnp.bfloat16)


def draw_local_keys(key, part):
    full_shape = (DOCS * QUERIES, HEADS * DH)
    drawn = jnp.clip(jax.random.normal(jax.random.fold_in(key, 22), full_shape, jnp.float32), -6.0, 6.0)
    return drawn.astype(jnp.bfloat16)


def touch_ends(result, rng, low, top_value):
    spot = [jax.random.randint(jax.random.fold_in(rng, axis), (), 0, length) for axis, length in enumerate(result.shape)]
    main_axis = result.shape.index(max(result.shape))
    neighbour = spot[:main_axis] + [(spot[main_axis] + 1) % result.shape[main_axis]] + spot[main_axis + 1:]
    return result.at[tuple(spot)].set(low).at[tuple(neighbour)].set(top_value)


def levels(own_key, extent, split, least, top_value):
    loudness, own = 1.0, jax.random.fold_in(own_key, 6)
    for axis_at, blocks in split:
        draws = jnp.exp(jax.random.uniform(jax.random.fold_in(own, axis_at), (blocks,), jnp.float32, least / len(split), top_value / len(split)))
        loudness = loudness * jnp.repeat(draws, extent[axis_at] // blocks).reshape([-1 if axis == axis_at else 1 for axis in range(len(extent))])
    return loudness


def normal_values(own_key, extent, width, limit, shards=(), kind=jnp.bfloat16):
    values = jax.random.normal(own_key, extent, jnp.float32) * width
    if len(shards) > 0:
        values = levels(own_key, extent, shards, -0.22, 0.18) * values
    return jnp.clip(values, min=-limit, max=limit).astype(kind)


def setup_inputs(seed: int = 0) -> dict:
    keys = jax.random.split(jax.random.key(seed), 9)
    queries = draw_queries(jax.random.fold_in(keys[8], 71), 0)
    local_keys = draw_local_keys(jax.random.fold_in(keys[8], 71), 0)
    local_values = normal_values(keys[2], (DOCS * QUERIES, HEADS * DH), 1.0, 6.0, ((0, 16), (1, 2)))
    mem_keys = normal_values(keys[3], (DOCS * MEM, HEADS * DH), 1.0, 6.0, ((0, 16), (1, 2)))
    mem_values = normal_values(keys[4], (DOCS * MEM, HEADS * DH), 1.0, 6.0, ((0, 16), (1, 2)))
    offsets = touch_ends(jax.random.randint(keys[5], (DOCS, SLOTS), 1, SLOTS + 1), jax.random.fold_in(keys[5], 1), 1, SLOTS).astype(jnp.int32)
    mem_lengths = touch_ends(jax.random.randint(keys[6], (DOCS,), 1, MEM + 1), jax.random.fold_in(keys[6], 1), 1, MEM).astype(jnp.int32)
    out_weight = normal_values(keys[7], (HEADS * DH, OUT), (HEADS * DH) ** -0.5, 0.09375, ((0, 2),))
    return {"queries": queries, "local_keys": local_keys, "local_values": local_values, "mem_keys": mem_keys, "mem_values": mem_values, "offsets": offsets, "mem_lengths": mem_lengths, "out_weight": out_weight}


def reference(queries, local_keys, local_values, mem_keys, mem_values, offsets, mem_lengths, out_weight):
    feature_width = HEADS * DH
    score_scale = 1.0 / math.sqrt(DH)
    query_rows = queries.reshape(DOCS, QUERIES, HEADS, DH)
    key_rows = local_keys.reshape(DOCS, QUERIES, HEADS, DH)
    value_rows = local_values.reshape(DOCS, QUERIES, HEADS, DH)
    memory_keys = mem_keys.reshape(DOCS, MEM, HEADS, DH)
    memory_values = mem_values.reshape(DOCS, MEM, HEADS, DH)
    causal = jnp.arange(QUERIES)[:, None] >= jnp.arange(QUERIES)[None, :]
    memory_index = jnp.arange(MEM)

    def one_doc(document):
        source = ((document - offsets[document]) % DOCS).astype(jnp.int32)
        owners = jnp.concatenate([document[None].astype(jnp.int32), source]).astype(jnp.int32)
        all_keys = jnp.concatenate([key_rows[document], memory_keys[owners].reshape(-1, HEADS, DH)], axis=0)
        all_values = jnp.concatenate([value_rows[document], memory_values[owners].reshape(-1, HEADS, DH)], axis=0)
        live_rows = memory_index[None, :] < mem_lengths[owners][:, None]
        live_mask = jnp.concatenate([causal, jnp.broadcast_to(live_rows.reshape(1, -1), (QUERIES, (SLOTS + 1) * MEM))], axis=1)
        scores = jnp.einsum('qhd,khd->hqk', query_rows[document].astype(jnp.float32), all_keys.astype(jnp.float32)) * score_scale
        scores = jnp.where(live_mask[None], scores, -1e+30)
        row_max = lax.optimization_barrier(jnp.max(scores, axis=-1, keepdims=True))
        exponent = jnp.where(live_mask[None], jnp.exp(scores - row_max), 0.0)
        weights = (exponent / lax.optimization_barrier(jnp.sum(exponent, axis=-1, keepdims=True))).astype(jnp.bfloat16)
        head_out = jnp.einsum('hqk,khd->qhd', weights.astype(jnp.float32), all_values.astype(jnp.float32)).astype(jnp.bfloat16)
        return head_out.reshape(QUERIES, feature_width)
    attended = lax.map(one_doc, jnp.arange(DOCS).astype(jnp.int32)).reshape(DOCS * QUERIES, feature_width)
    return jnp.dot(attended, out_weight, preferred_element_type=jnp.float32).astype(jnp.bfloat16)
```

```python
import functools
import math

import jax
import jax.numpy as jnp
from jax import lax
from jax.experimental import pallas as pl
from jax.experimental.pallas import tpu as pltpu
from jax.sharding import PartitionSpec as P

DH = 128
SCALE = math.log2(math.e) / math.sqrt(DH)
NEVER = -1e30
CHUNKS = 4
ROWS = 256
HEADS_PER_STEP = 2
VMEM = 48 * 1024 * 1024


def nt_dot(a, b):
    return lax.dot_general(a, b, (((1,), (1,)), ((), ())), preferred_element_type=jnp.float32)


def attend(query, pieces):
    scores = []
    top = None
    for keys, _, live in pieces:
        score = nt_dot(query, keys)
        if live is not None:
            score = jnp.where(live, score, NEVER)
        scores.append(score)
        piece_top = jnp.max(score, axis=1, keepdims=True)
        top = piece_top if top is None else jnp.maximum(top, piece_top)
    total = None
    for score, (_, values, _) in zip(scores, pieces):
        weights = jnp.exp2((score - top) * SCALE).astype(jnp.bfloat16)
        wide = jnp.concatenate([values, jnp.ones_like(values)], axis=1)
        part = jnp.dot(weights, wide, preferred_element_type=jnp.float32)
        total = part if total is None else total + part
    summed = total[:, DH:]
    return total[:, :DH] / summed, top * SCALE + jnp.log2(summed)


def merge(parts):
    top = functools.reduce(jnp.maximum, [log for _, log in parts])
    shares = [jnp.exp2(log - top) for _, log in parts]
    whole = functools.reduce(jnp.add, shares)
    out = functools.reduce(jnp.add, [share * part for share, (part, _) in zip(shares, parts)])
    return out / whole, top + jnp.log2(whole)


def to_rows(row):
    return jnp.broadcast_to(row, (DH, row.shape[1])).T


def to_row(log):
    return log.T[0:1, :]


def memory_pieces(key_ref, value_ref, columns, size, block, length):
    pieces = []
    if size > block:
        rows = pl.ds(0, size - block)
        pieces.append((key_ref[rows, columns], value_ref[rows, columns], None))
    rows = pl.ds(size - block, block)
    index = lax.broadcasted_iota(jnp.int32, (1, block), 1) + (size - block)
    pieces.append((key_ref[rows, columns], value_ref[rows, columns], index < length))
    return pieces


def by_length(length, memory_rows, run):
    block = memory_rows // 4
    for step in range(1, 5):
        size = step * block
        low = length > size - block if step > 1 else True
        high = length <= size if step < 4 else True
        pl.when(jnp.logical_and(low, high))(functools.partial(run, size, block))


def near_kernel(heads, numbers, q_ref, lk_ref, lv_ref, mk_ref, mv_ref, o_ref, log_ref):
    length = numbers[0]
    count = q_ref.shape[0]

    def run(size, block):
        for head in range(heads):
            columns = pl.ds(head * DH, DH)
            for start in range(0, count, ROWS):
                rows = pl.ds(start, ROWS)
                pieces = memory_pieces(mk_ref, mv_ref, columns, size, block, length)
                if start:
                    past = pl.ds(0, start)
                    pieces.append((lk_ref[past, columns], lv_ref[past, columns], None))
                causal = lax.broadcasted_iota(jnp.int32, (ROWS, ROWS), 0) >= (
                    lax.broadcasted_iota(jnp.int32, (ROWS, ROWS), 1)
                )
                pieces.append((lk_ref[rows, columns], lv_ref[rows, columns], causal))
                out, log = attend(q_ref[rows, columns], pieces)
                o_ref[rows, columns] = out.astype(o_ref.dtype)
                log_ref[head, :, rows] = to_row(log)

    by_length(length, mk_ref.shape[0], run)


def visit_kernel(heads, extra, numbers, q_ref, mk_ref, mv_ref, *refs):
    parts, (o_ref, log_ref) = refs[: 2 * extra], refs[2 * extra :]
    length, uses = numbers[0], numbers[1]
    count = q_ref.shape[0]

    def others(head, rows, columns):
        return [
            (parts[2 * at][rows, columns].astype(jnp.float32), to_rows(parts[2 * at + 1][head, :, rows]))
            for at in range(extra)
        ]

    def run(size, block):
        bonus = jnp.log2(jnp.full((ROWS, DH), uses, jnp.int32).astype(jnp.float32))
        for head in range(heads):
            columns = pl.ds(head * DH, DH)
            for start in range(0, count, ROWS):
                rows = pl.ds(start, ROWS)
                pieces = memory_pieces(mk_ref, mv_ref, columns, size, block, length)
                out, log = attend(q_ref[rows, columns], pieces)
                log = log + bonus
                if extra:
                    out, log = merge([(out, log)] + others(head, rows, columns))
                o_ref[rows, columns] = out.astype(o_ref.dtype)
                log_ref[head, :, rows] = to_row(log)

    @pl.when(uses > 0)
    def _():
        by_length(length, mk_ref.shape[0], run)

    @pl.when(uses == 0)
    def _():
        for head in range(heads):
            columns = pl.ds(head * DH, DH)
            for start in range(0, count, ROWS):
                rows = pl.ds(start, ROWS)
                if extra:
                    out, log = merge(others(head, rows, columns))
                    o_ref[rows, columns] = out.astype(o_ref.dtype)
                    log_ref[head, :, rows] = to_row(log)
                else:
                    o_ref[rows, columns] = jnp.zeros((ROWS, DH), o_ref.dtype)
                    log_ref[head, :, rows] = jnp.full((1, ROWS), NEVER, jnp.float32)


def final_kernel(heads, extra, *refs):
    o_ref = refs[-1]
    for head in range(heads):
        columns = pl.ds(head * DH, DH)
        for start in range(0, o_ref.shape[0], ROWS):
            rows = pl.ds(start, ROWS)
            parts = [
                (refs[2 * at][rows, columns].astype(jnp.float32), to_rows(refs[2 * at + 1][head, :, rows]))
                for at in range(extra)
            ]
            o_ref[rows, columns] = merge(parts)[0].astype(o_ref.dtype)


def per_device(
    queries, local_keys, local_values, mem_keys, mem_values, offsets, mem_lengths, out_weight
):
    count, width = queries.shape
    local_heads = width // DH
    memory_rows = mem_keys.shape[0]
    slots = offsets.shape[1]
    documents = lax.axis_size("doc")
    document = lax.axis_index("doc")
    core = document % 2
    side = (document // 2) % 2
    chunks = min(CHUNKS, local_heads)
    chunk_heads = local_heads // chunks
    heads = min(HEADS_PER_STEP, chunk_heads)
    steps = chunk_heads // heads
    block = heads * DH

    def permuted(values, target):
        pairs = [(source, target(source)) for source in range(documents)]
        return jax.tree.map(lambda value: lax.ppermute(value, "doc", pairs), values)

    down = lambda source: (source - slots) % documents
    up = lambda source: (source + slots) % documents
    across = lambda source: source ^ 2
    beside = lambda source: source ^ 1

    length = lax.dynamic_index_in_dim(mem_lengths, document, keepdims=False)
    table = lax.all_gather(offsets, "doc", axis=0, tiled=True)

    def numbers(distance):
        row = lax.dynamic_index_in_dim(table, (document + distance) % documents, keepdims=False)
        return jnp.stack([length, jnp.sum((row == distance).astype(jnp.int32))]).astype(jnp.int32)

    smem = pl.BlockSpec(memory_space=pltpu.SMEM)
    params = pltpu.CompilerParams(vmem_limit_bytes=VMEM)

    def flat(chunk, rows):
        return pl.BlockSpec((rows, block), lambda i: (0, chunk * steps + i))

    log_spec = pl.BlockSpec((heads, 1, count), lambda i: (i, 0, 0))
    part_shape = (
        jax.ShapeDtypeStruct((count, chunk_heads * DH), jnp.bfloat16),
        jax.ShapeDtypeStruct((chunk_heads, 1, count), jnp.float32),
    )
    part_specs = (flat(0, count), log_spec)

    def cost(keys):
        return pl.CostEstimate(
            flops=4 * count * keys * DH * chunk_heads * 2,
            bytes_accessed=4 * (count + keys) * DH * chunk_heads,
            transcendentals=count * keys * chunk_heads,
        )

    def near(chunk):
        return pl.pallas_call(
            functools.partial(near_kernel, heads),
            grid=(steps,),
            in_specs=[smem] + [flat(chunk, count)] * 3 + [flat(chunk, memory_rows)] * 2,
            out_specs=part_specs,
            out_shape=part_shape,
            compiler_params=params,
            cost_estimate=cost(count + memory_rows),
        )(length[None], queries, local_keys, local_values, mem_keys, mem_values)

    def visit(chunk, scalars, visiting, *parts):
        return pl.pallas_call(
            functools.partial(visit_kernel, heads, len(parts)),
            grid=(steps,),
            in_specs=[smem, flat(0, count)]
            + [flat(chunk, memory_rows)] * 2
            + list(part_specs) * len(parts),
            out_specs=part_specs,
            out_shape=part_shape,
            compiler_params=params,
            cost_estimate=cost(memory_rows),
        )(scalars, visiting, mem_keys, mem_values, *[x for part in parts for x in part])

    def final(*parts):
        return pl.pallas_call(
            functools.partial(final_kernel, heads, len(parts)),
            grid=(steps,),
            in_specs=list(part_specs) * len(parts),
            out_specs=part_specs[0],
            out_shape=part_shape[0],
            compiler_params=params,
            cost_estimate=pl.CostEstimate(
                flops=10 * count * chunk_heads * DH,
                bytes_accessed=2 * (len(parts) + 1) * count * chunk_heads * DH,
                transcendentals=4 * count * chunk_heads * DH,
            ),
        )(*[x for part in parts for x in part])

    def only(part, condition):
        return part[0], jnp.where(condition, part[1], NEVER)

    far = numbers(slots)
    middle = numbers(2)
    first = numbers(jnp.where(core == 0, 3, 1))
    second = numbers(jnp.where(core == 0, 1, 3))

    own = [queries[:, c * chunk_heads * DH : (c + 1) * chunk_heads * DH] for c in range(chunks)]
    ahead = [permuted(own[c], down) for c in range(chunks)]
    nears = [near(c) for c in range(chunks)]
    attended = []
    for c in range(chunks):
        swapped = permuted(jnp.where(side == 0, ahead[c], own[c]), across)
        visitor_one = permuted(swapped, beside)
        visitor_two = permuted(jnp.where(core == 0, ahead[c], own[c]), beside)
        back_one = permuted(visit(c, first, visitor_one), beside)
        back_two = permuted(visit(c, second, visitor_two), beside)
        back_across = permuted(visit(c, middle, swapped, back_one), across)
        back_far = permuted(
            visit(c, far, ahead[c], only(back_two, core == 0), only(back_across, side == 0)), up
        )
        attended.append(
            final(nears[c], back_far, only(back_two, core == 1), only(back_across, side == 1))
        )
    mixed = jnp.dot(
        jnp.concatenate(attended, axis=1), out_weight, preferred_element_type=jnp.float32
    )
    if lax.axis_size("head") != 2:
        return lax.psum_scatter(
            mixed.astype(jnp.bfloat16), "head", scatter_dimension=0, tiled=True
        )
    half = count // 2
    place = lax.axis_index("head")
    kept = lax.dynamic_slice_in_dim(mixed, place * half, half, 0)
    sent = lax.dynamic_slice_in_dim(mixed, (1 - place) * half, half, 0).astype(jnp.bfloat16)
    received = lax.ppermute(sent, "head", [(0, 1), (1, 0)])
    return (kept + received.astype(jnp.float32)).astype(jnp.bfloat16)


def solution(mesh):
    in_specs = (
        P("doc", "head"),
        P("doc", "head"),
        P("doc", "head"),
        P("doc", "head"),
        P("doc", "head"),
        P("doc", None),
        P(),
        P("head", None),
    )
    out_specs = P(("doc", "head"), None)
    return jax.shard_map(
        per_device, mesh=mesh, in_specs=in_specs, out_specs=out_specs, check_vma=False
    )
```

```python
import functools
import math

import jax
import jax.numpy as jnp
from jax import lax
from jax.experimental import pallas as pl
from jax.experimental.pallas import tpu as pltpu
from jax.sharding import PartitionSpec as P

DH = 128
SCALE = math.log2(math.e) / math.sqrt(DH)
NEVER = -1e30
CHUNKS = 4
ROWS = 256
HEADS_PER_STEP = 2
VMEM = 48 * 1024 * 1024


def nt_dot(a, b):
    return lax.dot_general(a, b, (((1,), (1,)), ((), ())), preferred_element_type=jnp.float32)


def attend(query, pieces):
    scores = []
    top = None
    for keys, _, live in pieces:
        score = nt_dot(query, keys)
        if live is not None:
            score = jnp.where(live, score, NEVER)
        scores.append(score)
        piece_top = jnp.max(score, axis=1, keepdims=True)
        top = piece_top if top is None else jnp.maximum(top, piece_top)
    total = None
    for score, (_, values, _) in zip(scores, pieces):
        weights = jnp.exp2((score - top) * SCALE).astype(jnp.bfloat16)
        wide = jnp.concatenate([values, jnp.ones_like(values)], axis=1)
        part = jnp.dot(weights, wide, preferred_element_type=jnp.float32)
        total = part if total is None else total + part
    summed = total[:, DH:]
    return total[:, :DH] / summed, top * SCALE + jnp.log2(summed)


def merge(parts):
    top = functools.reduce(jnp.maximum, [log for _, log in parts])
    shares = [jnp.exp2(log - top) for _, log in parts]
    whole = functools.reduce(jnp.add, shares)
    out = functools.reduce(jnp.add, [share * part for share, (part, _) in zip(shares, parts)])
    return out / whole, top + jnp.log2(whole)


def pack(logs, extra_rows):
    lines = []
    for log in logs:
        row = log.T[0:1, :]
        lines += [row[:, at : at + DH] for at in range(0, row.shape[1], DH)]
    rest = jnp.concatenate(lines, axis=0)
    parts = []
    for _ in range(3):
        part = rest.astype(jnp.bfloat16).astype(jnp.float32)
        parts.append(part)
        rest = rest - part
    spare = extra_rows - 3 * len(lines)
    if spare:
        parts.append(jnp.zeros((spare, DH), jnp.float32))
    return jnp.concatenate(parts, axis=0).astype(jnp.bfloat16)


def unpack(ref, count, columns, start):
    lines = count // DH
    parts = ref[pl.ds(count, ref.shape[0] - count), columns].astype(jnp.float32)
    logs = parts[:lines] + parts[lines : 2 * lines] + parts[2 * lines : 3 * lines]
    at = start // DH
    blocks = [
        jnp.broadcast_to(logs[line : line + 1], (DH, DH)).T for line in range(at, at + ROWS // DH)
    ]
    return jnp.concatenate(blocks, axis=0)


def read_part(ref, count, columns, start, penalty):
    log = unpack(ref, count, columns, start)
    if penalty is not None:
        log = log + penalty
    return ref[pl.ds(start, ROWS), columns].astype(jnp.float32), log


def penalty_of(flag):
    return jnp.where(flag > 0, 0.0, NEVER)


def memory_pieces(key_ref, value_ref, columns, size, block, length):
    pieces = []
    if size > block:
        rows = pl.ds(0, size - block)
        pieces.append((key_ref[rows, columns], value_ref[rows, columns], None))
    rows = pl.ds(size - block, block)
    index = lax.broadcasted_iota(jnp.int32, (1, block), 1) + (size - block)
    pieces.append((key_ref[rows, columns], value_ref[rows, columns], index < length))
    return pieces


def by_length(length, memory_rows, run):
    block = memory_rows // 4
    for step in range(1, 5):
        size = step * block
        low = length > size - block if step > 1 else True
        high = length <= size if step < 4 else True
        pl.when(jnp.logical_and(low, high))(functools.partial(run, size, block))


def near_kernel(heads, numbers, _, q_ref, lk_ref, lv_ref, mk_ref, mv_ref, o_ref):
    length = numbers[0]
    count = q_ref.shape[0]
    extra_rows = o_ref.shape[0] - count

    def run(size, block):
        for head in range(heads):
            columns = pl.ds(head * DH, DH)
            logs = []
            for start in range(0, count, ROWS):
                rows = pl.ds(start, ROWS)
                pieces = memory_pieces(mk_ref, mv_ref, columns, size, block, length)
                if start:
                    past = pl.ds(0, start)
                    pieces.append((lk_ref[past, columns], lv_ref[past, columns], None))
                causal = lax.broadcasted_iota(jnp.int32, (ROWS, ROWS), 0) >= (
                    lax.broadcasted_iota(jnp.int32, (ROWS, ROWS), 1)
                )
                pieces.append((lk_ref[rows, columns], lv_ref[rows, columns], causal))
                out, log = attend(q_ref[rows, columns], pieces)
                o_ref[rows, columns] = out.astype(o_ref.dtype)
                logs.append(log)
            o_ref[pl.ds(count, extra_rows), columns] = pack(logs, extra_rows)

    by_length(length, mk_ref.shape[0], run)


def visit_kernel(heads, flagged, numbers, _, q_ref, mk_ref, mv_ref, *refs):
    parts, o_ref = refs[:-1], refs[-1]
    length = numbers[0]
    uses = numbers[1] if parts else numbers[1 + pl.program_id(1)]
    count = q_ref.shape[0]
    extra_rows = o_ref.shape[0] - count

    def others(columns, start):
        return [
            read_part(
                ref, count, columns, start, penalty_of(numbers[2 + at]) if flagged else None
            )
            for at, ref in enumerate(parts)
        ]

    def run(size, block):
        bonus = jnp.log2(jnp.full((ROWS, DH), uses, jnp.int32).astype(jnp.float32))
        for head in range(heads):
            columns = pl.ds(head * DH, DH)
            logs = []
            for start in range(0, count, ROWS):
                rows = pl.ds(start, ROWS)
                pieces = memory_pieces(mk_ref, mv_ref, columns, size, block, length)
                out, log = attend(q_ref[rows, columns], pieces)
                log = log + bonus
                if parts:
                    out, log = merge([(out, log)] + others(columns, start))
                o_ref[rows, columns] = out.astype(o_ref.dtype)
                logs.append(log)
            o_ref[pl.ds(count, extra_rows), columns] = pack(logs, extra_rows)

    @pl.when(uses > 0)
    def _():
        by_length(length, mk_ref.shape[0], run)

    @pl.when(uses == 0)
    def _():
        for head in range(heads):
            columns = pl.ds(head * DH, DH)
            logs = []
            for start in range(0, count, ROWS):
                out, log = jnp.zeros((ROWS, DH), jnp.float32), jnp.full((ROWS, DH), NEVER)
                if parts:
                    out, log = merge(others(columns, start))
                o_ref[pl.ds(start, ROWS), columns] = out.astype(o_ref.dtype)
                logs.append(log)
            o_ref[pl.ds(count, extra_rows), columns] = pack(logs, extra_rows)


def final_kernel(heads, flags, numbers, _, *refs):
    parts, o_ref = refs[:-1], refs[-1]
    count = o_ref.shape[0]
    for head in range(heads):
        columns = pl.ds(head * DH, DH)
        for start in range(0, count, ROWS):
            read = [
                read_part(
                    ref,
                    count,
                    columns,
                    start,
                    None if flag is None else penalty_of(numbers[flag]),
                )
                for ref, flag in zip(parts, flags)
            ]
            o_ref[pl.ds(start, ROWS), columns] = merge(read)[0].astype(o_ref.dtype)


def per_device(
    queries, local_keys, local_values, mem_keys, mem_values, offsets, mem_lengths, out_weight
):
    count, width = queries.shape
    local_heads = width // DH
    memory_rows = mem_keys.shape[0]
    slots = offsets.shape[1]
    documents = lax.axis_size("doc")
    document = lax.axis_index("doc")
    core = document % 2
    side = (document // 2) % 2
    chunks = min(CHUNKS, local_heads)
    chunk_heads = local_heads // chunks
    heads = min(HEADS_PER_STEP, chunk_heads)
    steps = chunk_heads // heads
    block = heads * DH

    def permuted(values, target):
        pairs = [(source, target(source)) for source in range(documents)]
        return jax.tree.map(lambda value: lax.ppermute(value, "doc", pairs), values)

    down = lambda source: (source - slots) % documents
    up = lambda source: (source + slots) % documents
    across = lambda source: source ^ 2
    beside = lambda source: source ^ 1

    length = lax.dynamic_index_in_dim(mem_lengths, document, keepdims=False)

    def uses_at(distance):
        row = permuted(offsets, lambda source: (source - distance) % documents)
        return jnp.sum((row == distance).astype(jnp.int32))

    def whole_numbers(*values):
        return jnp.stack([jnp.asarray(value, jnp.int32) for value in values])

    smem = pl.BlockSpec(memory_space=pltpu.SMEM)
    unread = pl.BlockSpec(memory_space=pl.ANY)
    params = pltpu.CompilerParams(vmem_limit_bytes=VMEM)
    chunk_width = chunk_heads * DH
    extra_rows = -(-3 * (count // DH) // 16) * 16
    packed = count + extra_rows

    def flat(chunk, rows):
        return pl.BlockSpec((rows, block), lambda i: (0, chunk * steps + i))

    part_shape = jax.ShapeDtypeStruct((packed, chunk_width), jnp.bfloat16)
    latest = queries

    def cost(keys):
        return pl.CostEstimate(
            flops=4 * count * keys * DH * chunk_heads * 2,
            bytes_accessed=4 * (count + keys) * DH * chunk_heads,
            transcendentals=count * keys * chunk_heads,
        )

    def near(chunk):
        return pl.pallas_call(
            functools.partial(near_kernel, heads),
            grid=(steps,),
            in_specs=[smem, unread] + [flat(chunk, count)] * 3 + [flat(chunk, memory_rows)] * 2,
            out_specs=flat(0, packed),
            out_shape=part_shape,
            compiler_params=params,
            cost_estimate=cost(count + memory_rows),
        )(length[None], latest, queries, local_keys, local_values, mem_keys, mem_values)

    def visit_pair(chunk, scalars, visiting):
        memory = pl.BlockSpec((memory_rows, block), lambda i, v: (0, chunk * steps + i))
        return pl.pallas_call(
            functools.partial(visit_kernel, heads, False),
            grid=(steps, 2),
            in_specs=[smem, unread, pl.BlockSpec((count, block), lambda i, v: (v, i))]
            + [memory] * 2,
            out_specs=pl.BlockSpec((None, packed, block), lambda i, v: (v, 0, i)),
            out_shape=jax.ShapeDtypeStruct((2, packed, chunk_width), jnp.bfloat16),
            compiler_params=params,
            cost_estimate=cost(2 * memory_rows),
        )(scalars, latest, visiting, mem_keys, mem_values)

    def spec_at(at):
        return pl.BlockSpec((None, packed, block), lambda i: (at, 0, i))

    def visit(chunk, scalars, visiting, flagged, parts, specs):
        return pl.pallas_call(
            functools.partial(visit_kernel, heads, flagged),
            grid=(steps,),
            in_specs=[smem, unread, flat(0, count)] + [flat(chunk, memory_rows)] * 2 + specs,
            out_specs=flat(0, packed),
            out_shape=part_shape,
            compiler_params=params,
            cost_estimate=cost(memory_rows),
        )(scalars, latest, visiting, mem_keys, mem_values, *parts)

    def final(scalars, flags, parts, specs):
        return pl.pallas_call(
            functools.partial(final_kernel, heads, flags),
            grid=(steps,),
            in_specs=[smem, unread] + specs,
            out_specs=flat(0, count),
            out_shape=jax.ShapeDtypeStruct((count, chunk_width), jnp.bfloat16),
            compiler_params=params,
            cost_estimate=pl.CostEstimate(
                flops=10 * count * chunk_width,
                bytes_accessed=2 * (len(parts) + 1) * count * chunk_width,
                transcendentals=4 * count * chunk_width,
            ),
        )(scalars, latest, *parts)

    own = [queries[:, c * chunk_width : (c + 1) * chunk_width] for c in range(chunks)]
    ahead = [permuted(own[c], down) for c in range(chunks)]
    pair_of_heads = lax.axis_size("head") == 2
    swap_head = lambda value: lax.ppermute(value, "head", [(0, 1), (1, 0)])
    uses = [uses_at(distance) for distance in (1, 2, 3, 4)]
    is_core, is_side = (core == 0).astype(jnp.int32), (side == 0).astype(jnp.int32)
    pair_numbers = whole_numbers(
        length, jnp.where(core == 0, uses[2], uses[0]), jnp.where(core == 0, uses[0], uses[2])
    )
    middle_numbers = whole_numbers(length, uses[1])
    far_numbers = whole_numbers(length, uses[3], is_core, is_side)
    final_numbers = whole_numbers(1 - is_core, 1 - is_side)

    swapped, pairs_in = [], []
    for c in range(chunks):
        swapped.append(permuted(jnp.where(side == 0, ahead[c], own[c]), across))
        other = jnp.where(core == 0, ahead[c], own[c])
        pairs_in.append(permuted(jnp.concatenate([swapped[c], other], axis=0), beside))

    nears, backs, backs_across, backs_far = {}, {}, {}, {}
    attended, arrived = {}, {}
    half = count // 2
    place = lax.axis_index("head")

    def step(kind, c):
        nonlocal latest
        if kind == "near":
            latest = nears[c] = near(c)
        elif kind == "pair":
            latest = visit_pair(c, pair_numbers, pairs_in[c])
            backs[c] = permuted(latest, beside)
        elif kind == "middle":
            latest = visit(c, middle_numbers, swapped[c], False, [backs[c]], [spec_at(0)])
            backs_across[c] = permuted(latest, across)
        elif kind == "far":
            latest = visit(
                c,
                far_numbers,
                ahead[c],
                True,
                [backs[c], backs_across[c]],
                [spec_at(1), flat(0, packed)],
            )
            backs_far[c] = permuted(latest, up)
        else:
            latest = attended[c] = final(
                final_numbers,
                (None, None, 0, 1),
                [nears[c], backs_far[c], backs[c], backs_across[c]],
                [flat(0, packed), flat(0, packed), spec_at(1), flat(0, packed)],
            )
            if pair_of_heads:
                arrived[c] = swap_head(
                    lax.dynamic_slice_in_dim(attended[c], (1 - place) * half, half, 0)
                )

    lags = (("near", 0), ("pair", chunks), ("middle", chunks + 2), ("far", chunks + 4))
    plan = []
    for c in range(chunks):
        for kind, lag in lags:
            plan.append((c + lag, -lag, kind, c))
        plan.append((max(c + chunks + 6, 2 * chunks + 2.5), 0, "final", c))
    for _, _, kind, c in sorted(plan):
        step(kind, c)

    every = range(chunks)
    full = jnp.concatenate([attended[c] for c in every], axis=1)
    if not pair_of_heads:
        mixed = jnp.dot(full, out_weight, preferred_element_type=jnp.float32)
        return lax.psum_scatter(
            mixed.astype(jnp.bfloat16), "head", scatter_dimension=0, tiled=True
        )
    depth = out_weight.shape[0] // 2
    mine = swap_head(lax.dynamic_slice_in_dim(out_weight, core * depth, depth, 0))
    others = permuted(mine, beside)
    kept = lax.dynamic_slice_in_dim(full, place * half, half, 0)
    came = jnp.concatenate([arrived[c] for c in every], axis=1)
    mixed = jnp.dot(kept, out_weight, preferred_element_type=jnp.float32)
    for part, at in ((mine, core), (others, 1 - core)):
        mixed = mixed + jnp.dot(
            lax.dynamic_slice_in_dim(came, at * depth, depth, 1),
            part,
            preferred_element_type=jnp.float32,
        )
    return mixed.astype(jnp.bfloat16)


def solution(mesh):
    in_specs = (
        P("doc", "head"),
        P("doc", "head"),
        P("doc", "head"),
        P("doc", "head"),
        P("doc", "head"),
        P("doc", None),
        P(),
        P("head", None),
    )
    out_specs = P(("doc", "head"), None)
    return jax.shard_map(
        per_device, mesh=mesh, in_specs=in_specs, out_specs=out_specs, check_vma=False
    )
```
